32 devices in a mesh: groups: 2 (over x), row: 8 (over z, y), col: 2 (over core).
Axes of the slice: x: 2, y: 2, z: 4, core: 2. Of those that a mesh axis runs over, the one named last changes fastest.
Arguments:
- right_side: float32 [32, 4096], P('groups', ('row', 'col')), parts along dimension 0, may hold values from -6 to 6
- current_ratio: float32 [8192], P(('groups', 'row', 'col')), parts along dimension 0, may hold values from 0.7 to 1
- filament_xy: float32 [2, 6400], replicated, may hold values from -0.3 to 0.3
- element_offset: float32 [2, 8192], P(None, 'groups'), parts along dimension 1, may hold values from -0.003 to 0.003
- element_filament: int32 [8192], P('groups'), parts along dimension 0, may hold values from 0 to 6399
- element_order: int32 [8192], P('groups'), parts along dimension 0, may hold values from 0 to 4095, each once
Outputs:
- solution: float32 [32, 4096], P('groups', ('row', 'col')), parts along dimension 0
- residual: float32 [32, 4096], P('groups', ('row', 'col')), parts along dimension 0
The draws below stay inside these ranges and needn't reach their ends.
There are 2 independent parts, one for each index of `groups`. The reference program is written for one: setup_inputs(seed, part) draws one part's arguments, and reference() takes and returns one part's arrays. A program takes and returns all parts, laid end to end along the dimension named above; an argument that names none is the same for every part. Nothing has to cross between parts.
Inputs may be any that keep to these rules, and one draw needn't show every extreme that they name: `element_order`: each position appears once.
All inputs are finite; a program needn't handle non-finite values.
Results may differ from the reference program's by a relative error of at most 0.00014.
Values sent between devices are 32-bit elements; how exact they have to be, the bound alone decides.
A program may use at most 128 MiB of HBM per device.

```python
import math
import jax
import jax.numpy as jnp
from jax import lax

NRHS = 16
NF = 6400
ITERS = 2
N = 4096


def with_ends(entries, key, low, top_value):
    spot = [jax.random.randint(jax.random.fold_in(key, axis), (), 0, length) for axis, length in enumerate(entries.shape)]
    main_axis = entries.shape.index(max(entries.shape))
    beside = spot[:main_axis] + [(spot[main_axis] + 1) % entries.shape[main_axis]] + spot[main_axis + 1:]
    return entries.at[tuple(spot)].set(low).at[tuple(beside)].set(top_value)


def block_levels(own_key, extent, cuts, low, largest):
    loudness = 1.0
    for dim, shards_of in cuts:
        steps = jax.random.uniform(jax.random.fold_in(jax.random.fold_in(own_key, 6), dim), (shards_of,), jnp.float32, low / len(cuts), largest / len(cuts))
        loudness = loudness * jnp.repeat(jnp.exp(steps), extent[dim] // shards_of).reshape((-1,) + (1,) * (len(extent) - 1 - dim))
    return loudness


def gaussian(stream_key, dims, deviation, limit, split=(), kind=jnp.bfloat16):
    values = deviation * jax.random.normal(stream_key, dims, jnp.float32)
    if split:
        values = values * block_levels(stream_key, dims, split, -0.22, 0.18)
    return jnp.clip(values, -limit, limit).astype(kind)


def setup_inputs(seed: int = 0, part: int = 0) -> dict:
    key_list = jax.random.split(jax.random.key(seed), 7)
    own_keys = jax.random.split(jax.random.fold_in(key_list[6], part), 7)
    right_side = gaussian(own_keys[0], (NRHS, N), 1.0, 6.0, ((1, 16),), jnp.float32)
    current_ratio = jnp.clip(0.7 + 0.3 * jax.random.uniform(own_keys[1], (N,), jnp.float32) ** block_levels(own_keys[1], (N,), ((0, 16),), -0.2, 0.2), 0.7, 1.0)
    filament_xy = jnp.clip(jax.random.uniform(key_list[2], (2, NF), jnp.float32, -0.3, 0.3), -0.3, 0.3)
    element_offset = jnp.clip(jax.random.uniform(own_keys[3], (2, N), jnp.float32, -0.003, 0.003), -0.003, 0.003)
    element_filament = with_ends(jax.random.randint(own_keys[4], (N,), 0, NF), jax.random.fold_in(own_keys[4], 1), 0, NF - 1).astype(jnp.int32)
    element_order = jax.random.permutation(own_keys[5], N).astype(jnp.int32)
    return dict(right_side=right_side, current_ratio=current_ratio, filament_xy=filament_xy, element_offset=element_offset, element_filament=element_filament, element_order=element_order)


EPS_SQUARED = 0.0001
COUPLE = 0.3

def kernel(left_x, left_y, right_x, right_y):
    delta_x = left_x[:, None] - right_x[None, :]
    delta_y = left_y[:, None] - right_y[None, :]
    return lax.rsqrt(delta_x * delta_x + delta_y * delta_y + EPS_SQUARED)

def reference(right_side, current_ratio, filament_xy, element_offset, element_filament, element_order):
    element_count = right_side.shape[1]
    side_count = right_side.shape[0]
    filament_of = element_filament[element_order]
    places = filament_xy[:, filament_of] + element_offset[:, element_order]
    diagonal = 1.0 + 8.0 * current_ratio ** 24
    coupling_scale = COUPLE / math.sqrt(element_count)
    block_size = math.gcd(element_count, 512)
    block_places = places.reshape(2, element_count // block_size, block_size).transpose(1, 0, 2)

    def apply_operator(direction):

        def apply_block(block_xy):
            coupling = kernel(places[0], places[1], block_xy[0], block_xy[1])
            return jnp.dot(direction, coupling, precision=lax.Precision.HIGHEST, preferred_element_type=jnp.float32)
        parts = lax.map(apply_block, block_places)
        coupled = parts.transpose(1, 0, 2).reshape(side_count, element_count)
        return diagonal * direction + coupling_scale * coupled
    solution = jnp.zeros_like(right_side)
    residual = right_side
    direction = right_side
    norm_now = lax.optimization_barrier(jnp.sum(residual * residual, axis=1, keepdims=True))
    for iteration in range(ITERS):
        image_vec = apply_operator(direction)
        step_length = norm_now / lax.optimization_barrier(jnp.sum(direction * image_vec, axis=1, keepdims=True))
        solution = solution + step_length * direction
        residual = residual - step_length * image_vec
        norm_next = lax.optimization_barrier(jnp.sum(residual * residual, axis=1, keepdims=True))
        direction = residual + norm_next / norm_now * direction
        norm_now = norm_next
    return (solution, residual)
```

```python
import functools
import math

import jax
import jax.numpy as jnp
from jax import lax
from jax.experimental import pallas as pl
from jax.experimental.pallas import tpu as pltpu
from jax.sharding import PartitionSpec as P

EPS_SQUARED = 0.0001
COUPLE = 0.3
LANES = 128
MESH = pl.DeviceIdType.MESH


def loop(count, body):
    if count <= 16:
        for k in range(count):
            body(k)
    else:
        lax.fori_loop(0, count, lambda k, _: (body(k), 0)[1], 0)


def pick(table, index):
    rows, n = table.shape[0], index.shape[1]
    hot = (lax.broadcasted_iota(jnp.int32, (rows, n), 0) == (index >> 7)).astype(jnp.float32)
    taken = lax.dot_general(
        table.T, hot, (((1,), (0,)), ((), ())), precision=lax.Precision.HIGHEST, preferred_element_type=jnp.float32
    )
    lane = lax.broadcasted_iota(jnp.int32, (LANES, n), 0)
    return jnp.sum(jnp.where(lane == (index & (LANES - 1)), taken, 0.0), axis=0, keepdims=True)


def split(value):
    high = value.astype(jnp.bfloat16)
    low = (value - high.astype(jnp.float32)).astype(jnp.bfloat16)
    return high, low


def kernel(
    rows, cols, scale,
    b_ref, ratio_ref, xy_ref, offset_ref, filament_ref, order_ref,
    solution_ref, residual_ref,
    offset_tab, xy_tab, near, b_all, xy_all, image_all, r_all, dots,
    send_b, recv_b, send_xy, recv_xy, send_im, recv_im, send_dot, recv_dot,
):
    count = rows * cols
    side, width = b_ref.shape
    group = lax.axis_index("groups")
    me = lax.axis_index("row") * cols + lax.axis_index("col")

    def peer(off):
        return lax.rem(me + off, count)

    def device(p):
        return (group, p // cols, lax.rem(p, cols))

    def copy(src, dst_all, send, recv, off):
        return pltpu.make_async_remote_copy(
            src_ref=src, dst_ref=dst_all.at[me], send_sem=send.at[off - 1], recv_sem=recv.at[me],
            device_id=device(peer(off)), device_id_type=MESH,
        )

    def arrived(dst_all, send, recv, p):
        pltpu.make_async_remote_copy(
            src_ref=dst_all.at[p], dst_ref=dst_all.at[p], send_sem=send.at[0], recv_sem=recv.at[p],
            device_id=device(peer(1)), device_id_type=MESH,
        ).wait_recv()

    barrier = pltpu.get_barrier_semaphore()
    loop(count - 1, lambda k: pl.semaphore_signal(barrier, inc=1, device_id=device(peer(k + 1)), device_id_type=MESH))

    for ref, tab in ((offset_ref, offset_tab), (xy_ref, xy_tab)):
        for axis in range(2):
            for q in range(ref.shape[1] // LANES):
                tab[axis, q : q + 1, :] = ref[axis : axis + 1, q * LANES : (q + 1) * LANES]
    parts = width // LANES
    order = jnp.concatenate([order_ref[pl.ds(me * parts + k, 1), :] for k in range(parts)], axis=1)
    filament = (pick(filament_ref[...].astype(jnp.float32), order) + 0.5).astype(jnp.int32)
    for axis in range(2):
        place = pick(xy_tab[axis], filament) + pick(offset_tab[axis], order)
        xy_all[me, axis : axis + 1, :] = place
        near[axis] = jnp.broadcast_to(place, (width, width)).T
    b_all[me] = b_ref[...]

    pl.semaphore_wait(barrier, count - 1)
    loop(count - 1, lambda k: copy(xy_all.at[me], xy_all, send_xy, recv_xy, k + 1).start())
    loop(count - 1, lambda k: copy(b_ref, b_all, send_b, recv_b, k + 1).start())

    ratio = ratio_ref[...]
    cube = ratio * ratio * ratio
    sixth = cube * cube
    twelfth = sixth * sixth
    diagonal = 1.0 + 8.0 * (twelfth * twelfth)

    def term(p, vector, total):
        dx = near[0] - xy_all[p, 0:1, :]
        dy = near[1] - xy_all[p, 1:2, :]
        coupling = lax.rsqrt(dx * dx + dy * dy + EPS_SQUARED)
        c_high, c_low = split(coupling)
        v_high, v_low = split(vector)
        contract = (((1,), (1,)), ((), ()))
        both = lax.dot_general(
            jnp.concatenate([v_high, v_low], axis=0), c_high, contract, preferred_element_type=jnp.float32
        )
        rest = lax.dot_general(v_high, c_low, contract, preferred_element_type=jnp.float32)
        return total + both[:side] + (both[side:] + rest)

    zero = jnp.zeros((side, width), jnp.float32)

    def rowsum(value):
        return jnp.sum(value, axis=1, keepdims=True)

    b = b_ref[...]
    total = term(me, b, zero)

    def first(k, carry):
        total, squares = carry
        p = peer(k)
        arrived(xy_all, send_xy, recv_xy, p)
        arrived(b_all, send_b, recv_b, p)
        value = b_all[p]
        return term(p, value, total), squares + value * value

    total, squares = lax.fori_loop(1, count, first, (total, b * b))
    image = diagonal * b + scale * total
    image_all[me] = image
    loop(count - 1, lambda k: copy(image_all.at[me], image_all, send_im, recv_im, k + 1).start())
    norm = rowsum(squares)

    def curve(k, carry):
        p = peer(k)
        arrived(image_all, send_im, recv_im, p)
        return carry + b_all[p] * image_all[p]

    curved = rowsum(lax.fori_loop(1, count, curve, b * image))
    step = norm / curved

    def reduce_residual(k, carry):
        value = b_all[k] - step * image_all[k]
        r_all[k] = value
        return carry + value * value

    norm_next = rowsum(lax.fori_loop(0, count, reduce_residual, zero))
    beta = norm_next / norm

    def second(k, total):
        return term(k, r_all[k] + beta * b_all[k], total)

    total = lax.fori_loop(0, count, second, zero)
    residual = r_all[me]
    direction = residual + beta * b
    image2 = diagonal * direction + scale * total

    own = (
        lax.broadcasted_iota(jnp.int32, (side, LANES), 0) == lax.broadcasted_iota(jnp.int32, (side, LANES), 1)
    )
    partial = rowsum(direction * image2)
    dots[me] = jnp.sum(jnp.where(own, partial, 0.0), axis=0, keepdims=True)
    loop(count - 1, lambda k: copy(dots.at[me], dots, send_dot, recv_dot, k + 1).start())
    loop(count - 1, lambda k: arrived(dots, send_dot, recv_dot, peer(k + 1)))
    row = lax.fori_loop(0, count, lambda k, acc: acc + dots[k], jnp.zeros((1, LANES), jnp.float32))
    curved2 = rowsum(jnp.where(own, row, 0.0))
    step2 = norm_next / curved2
    solution_ref[...] = step * b + step2 * direction
    residual_ref[...] = residual - step2 * image2

    for src, dst, send, recv in (
        (b_ref, b_all, send_b, recv_b),
        (xy_all.at[me], xy_all, send_xy, recv_xy),
        (image_all.at[me], image_all, send_im, recv_im),
        (dots.at[me], dots, send_dot, recv_dot),
    ):
        loop(count - 1, lambda k: copy(src, dst, send, recv, k + 1).wait_send())


def solution(mesh):
    rows, cols = mesh.shape["row"], mesh.shape["col"]
    count = rows * cols

    def on_device(right_side, current_ratio, filament_xy, element_offset, element_filament, element_order):
        side, width = right_side.shape
        elements = width * count
        shape = jax.ShapeDtypeStruct((side, width), jnp.float32)
        vmem = pl.BlockSpec(memory_space=pltpu.VMEM)
        f32 = jnp.float32
        blocks = pltpu.VMEM((count, side, width), f32)
        return pl.pallas_call(
            functools.partial(kernel, rows, cols, COUPLE / math.sqrt(elements)),
            out_shape=(shape, shape),
            in_specs=[vmem] * 6,
            out_specs=(vmem, vmem),
            scratch_shapes=[
                pltpu.VMEM((2, elements // LANES, LANES), f32),
                pltpu.VMEM((2, filament_xy.shape[1] // LANES, LANES), f32),
                pltpu.VMEM((2, width, width), f32),
                blocks,
                pltpu.VMEM((count, 2, width), f32),
                blocks,
                blocks,
                pltpu.VMEM((count, 1, LANES), f32),
            ]
            + [pltpu.SemaphoreType.DMA((count,))] * 8,
            compiler_params=pltpu.CompilerParams(
                collective_id=0, has_side_effects=True, vmem_limit_bytes=24 * 1024 * 1024
            ),
        )(
            right_side,
            current_ratio.reshape(1, width),
            filament_xy,
            element_offset,
            element_filament.reshape(elements // LANES, LANES),
            element_order.reshape(elements // LANES, LANES),
        )

    return jax.shard_map(
        on_device,
        mesh=mesh,
        in_specs=(
            P("groups", ("row", "col")),
            P(("groups", "row", "col")),
            P(),
            P(None, "groups"),
            P("groups"),
            P("groups"),
        ),
        out_specs=(P("groups", ("row", "col")), P("groups", ("row", "col"))),
        check_vma=False,
    )
```

```python
import functools
import math

import jax
import jax.numpy as jnp
from jax import lax
from jax.experimental import pallas as pl
from jax.experimental.pallas import tpu as pltpu
from jax.sharding import PartitionSpec as P

EPS_SQUARED = 0.0001
COUPLE = 0.3
LANES = 128
MESH = pl.DeviceIdType.MESH


def loop(count, body):
    if count <= 16:
        for k in range(count):
            body(k)
    else:
        lax.fori_loop(0, count, lambda k, _: (body(k), 0)[1], 0)


def pick(table, index):
    rows, n = table.shape[0], index.shape[1]
    hot = (lax.broadcasted_iota(jnp.int32, (rows, n), 0) == (index >> 7)).astype(jnp.float32)
    taken = lax.dot_general(
        table.T, hot, (((1,), (0,)), ((), ())), precision=lax.Precision.HIGHEST, preferred_element_type=jnp.float32
    )
    lane = lax.broadcasted_iota(jnp.int32, (LANES, n), 0)
    return jnp.sum(jnp.where(lane == (index & (LANES - 1)), taken, 0.0), axis=0, keepdims=True)


def split(value):
    high = value.astype(jnp.bfloat16)
    low = (value - high.astype(jnp.float32)).astype(jnp.bfloat16)
    return high, low


def kernel(
    rows, cols, scale,
    b_hbm, ratio_hbm, xy_hbm, offset_hbm, filament_hbm, order_hbm,
    solution_ref, residual_ref,
    b_ref, ratio_ref, xy_ref, offset_ref, filament_ref, order_ref,
    offset_tab, xy_tab, near, b_all, xy_all, image_all, r_all, dots,
    load, send_b, recv_b, send_xy, recv_xy, send_im, recv_im, send_dot, recv_dot,
):
    count = rows * cols
    side, width = b_ref.shape
    group = lax.axis_index("groups")
    row, col = lax.axis_index("row"), lax.axis_index("col")
    me = row * cols + col

    loads = [
        pltpu.make_async_copy(src, dst, load.at[k])
        for k, (src, dst) in enumerate(
            (
                (order_hbm, order_ref), (filament_hbm, filament_ref), (offset_hbm, offset_ref),
                (xy_hbm, xy_ref), (b_hbm, b_ref), (ratio_hbm, ratio_ref),
            )
        )
    ]
    for one in loads:
        one.start()

    def row_at(k):
        return lax.rem(row + k, rows)

    def col_at(c):
        return lax.rem(col + c, cols)

    def device(p):
        return (group, p // cols, lax.rem(p, cols))

    def peer(k):
        return lax.rem(me + k, count)

    def push(src, dst, send, recv, device_id):
        return pltpu.make_async_remote_copy(
            src_ref=src, dst_ref=dst, send_sem=send, recv_sem=recv, device_id=device_id, device_id_type=MESH
        )

    def across(src, dst_all, send, recv, k):
        return push(src, dst_all.at[me], send.at[k], recv.at[me], (group, row_at(k), col))

    def beside(src, dst_all, send, recv, k, c):
        p = row_at(k) * cols + col
        src = dst_all.at[p] if src is None else src
        return push(src, dst_all.at[p], send.at[rows + k * cols + c], recv.at[p], (group, row, col_at(c)))

    def spread(src, dst_all, send, recv):
        loop(rows - 1, lambda k: across(src, dst_all, send, recv, k + 1).start())
        loop(cols - 1, lambda c: beside(src, dst_all, send, recv, 0, c + 1).start())

    def forward(dst_all, send, recv, k):
        arrived(dst_all, recv, row_at(k) * cols + col)
        for c in range(1, cols):
            beside(None, dst_all, send, recv, k, c).start()

    def arrived(dst_all, recv, p):
        push(dst_all.at[p], dst_all.at[p], send_b.at[0], recv.at[p], device(peer(1))).wait_recv()

    def sent(src, dst_all, send, recv):
        loop(rows - 1, lambda k: across(src, dst_all, send, recv, k + 1).wait_send())
        for c in range(1, cols):
            loop(rows, lambda k: beside(None, dst_all, send, recv, k, c).wait_send())

    barrier = pltpu.get_barrier_semaphore()
    loop(count - 1, lambda k: pl.semaphore_signal(barrier, inc=1, device_id=device(peer(k + 1)), device_id_type=MESH))

    for one in loads:
        one.wait()
    for ref, tab in ((offset_ref, offset_tab), (xy_ref, xy_tab)):
        for axis in range(2):
            for q in range(ref.shape[1] // LANES):
                tab[axis, q : q + 1, :] = ref[axis : axis + 1, q * LANES : (q + 1) * LANES]
    parts = width // LANES
    order = jnp.concatenate([order_ref[pl.ds(me * parts + k, 1), :] for k in range(parts)], axis=1)
    filament = (pick(filament_ref[...].astype(jnp.float32), order) + 0.5).astype(jnp.int32)
    places = [pick(xy_tab[axis], filament) + pick(offset_tab[axis], order) for axis in range(2)]
    for axis in range(2):
        xy_all[me, axis : axis + 1, :] = places[axis]
    b_all[me] = b_ref[...]

    pl.semaphore_wait(barrier, count - 1)
    spread(xy_all.at[me], xy_all, send_xy, recv_xy)
    spread(b_ref, b_all, send_b, recv_b)

    for axis in range(2):
        near[axis] = jnp.broadcast_to(places[axis], (width, width)).T
    ratio = ratio_ref[...]
    cube = ratio * ratio * ratio
    sixth = cube * cube
    twelfth = sixth * sixth
    diagonal = 1.0 + 8.0 * (twelfth * twelfth)

    def term(p, vector, total):
        dx = near[0] - xy_all[p, 0:1, :]
        dy = near[1] - xy_all[p, 1:2, :]
        coupling = lax.rsqrt(dx * dx + dy * dy + EPS_SQUARED)
        c_high, c_low = split(coupling)
        v_high, v_low = split(vector)
        contract = (((1,), (1,)), ((), ()))
        both = lax.dot_general(
            jnp.concatenate([v_high, v_low], axis=0), c_high, contract, preferred_element_type=jnp.float32
        )
        rest = lax.dot_general(v_high, c_low, contract, preferred_element_type=jnp.float32)
        return total + both[:side] + (both[side:] + rest)

    zero = jnp.zeros((side, width), jnp.float32)

    def rowsum(value):
        return jnp.sum(value, axis=1, keepdims=True)

    def other(k):
        return row_at(k // (cols - 1)) * cols + col_at(1 + lax.rem(k, cols - 1))

    others = rows * (cols - 1)

    b = b_ref[...]
    total = term(me, b, zero)

    def add_first(p, carry):
        total, squares = carry
        value = b_all[p]
        return term(p, value, total), squares + value * value

    def first(k, carry):
        forward(xy_all, send_xy, recv_xy, k)
        forward(b_all, send_b, recv_b, k)
        return add_first(row_at(k) * cols + col, carry)

    def first_other(k, carry):
        p = other(k)
        arrived(xy_all, recv_xy, p)
        arrived(b_all, recv_b, p)
        return add_first(p, carry)

    carry = lax.fori_loop(1, rows, first, (total, b * b))
    total, squares = lax.fori_loop(0, others, first_other, carry)
    image = diagonal * b + scale * total
    image_all[me] = image
    spread(image_all.at[me], image_all, send_im, recv_im)
    norm = rowsum(squares)

    def curve(k, carry):
        forward(image_all, send_im, recv_im, k)
        p = row_at(k) * cols + col
        return carry + b_all[p] * image_all[p]

    def curve_other(k, carry):
        p = other(k)
        arrived(image_all, recv_im, p)
        return carry + b_all[p] * image_all[p]

    carry = lax.fori_loop(1, rows, curve, b * image)
    curved = rowsum(lax.fori_loop(0, others, curve_other, carry))
    step = norm / curved

    def reduce_residual(k, carry):
        value = b_all[k] - step * image_all[k]
        r_all[k] = value
        return carry + value * value

    norm_next = rowsum(lax.fori_loop(0, count, reduce_residual, zero))
    beta = norm_next / norm

    def second(k, total):
        return term(k, r_all[k] + beta * b_all[k], total)

    total = lax.fori_loop(0, count, second, zero)
    residual = r_all[me]
    direction = residual + beta * b
    image2 = diagonal * direction + scale * total

    own = (
        lax.broadcasted_iota(jnp.int32, (side, LANES), 0) == lax.broadcasted_iota(jnp.int32, (side, LANES), 1)
    )
    partial = rowsum(direction * image2)
    dots[me] = jnp.sum(jnp.where(own, partial, 0.0), axis=0, keepdims=True)

    def give(k):
        return push(dots.at[me], dots.at[me], send_dot.at[k], recv_dot.at[me], device(peer(k)))

    loop(count - 1, lambda k: give(k + 1).start())
    loop(count - 1, lambda k: arrived(dots, recv_dot, peer(k + 1)))
    flat = lax.fori_loop(0, count, lambda k, acc: acc + dots[k], jnp.zeros((1, LANES), jnp.float32))
    curved2 = rowsum(jnp.where(own, flat, 0.0))
    step2 = norm_next / curved2
    solution_ref[...] = step * b + step2 * direction
    residual_ref[...] = residual - step2 * image2

    sent(b_ref, b_all, send_b, recv_b)
    sent(xy_all.at[me], xy_all, send_xy, recv_xy)
    sent(image_all.at[me], image_all, send_im, recv_im)
    loop(count - 1, lambda k: give(k + 1).wait_send())


def solution(mesh):
    rows, cols = mesh.shape["row"], mesh.shape["col"]
    count = rows * cols

    def on_device(right_side, current_ratio, filament_xy, element_offset, element_filament, element_order):
        side, width = right_side.shape
        elements = width * count
        shape = jax.ShapeDtypeStruct((side, width), jnp.float32)
        vmem = pl.BlockSpec(memory_space=pltpu.VMEM)
        f32 = jnp.float32
        blocks = pltpu.VMEM((count, side, width), f32)
        return pl.pallas_call(
            functools.partial(kernel, rows, cols, COUPLE / math.sqrt(elements)),
            out_shape=(shape, shape),
            in_specs=[pl.BlockSpec(memory_space=pltpu.HBM)] * 6,
            out_specs=(vmem, vmem),
            scratch_shapes=[
                pltpu.VMEM((side, width), f32),
                pltpu.VMEM((1, width), f32),
                pltpu.VMEM(filament_xy.shape, f32),
                pltpu.VMEM(element_offset.shape, f32),
                pltpu.VMEM((elements // LANES, LANES), jnp.int32),
                pltpu.VMEM((elements // LANES, LANES), jnp.int32),
                pltpu.VMEM((2, elements // LANES, LANES), f32),
                pltpu.VMEM((2, filament_xy.shape[1] // LANES, LANES), f32),
                pltpu.VMEM((2, width, width), f32),
                blocks,
                pltpu.VMEM((count, 2, width), f32),
                blocks,
                blocks,
                pltpu.VMEM((count, 1, LANES), f32),
            ]
            + [pltpu.SemaphoreType.DMA((6,))]
            + [pltpu.SemaphoreType.DMA((rows * (1 + cols),)), pltpu.SemaphoreType.DMA((count,))] * 4,
            compiler_params=pltpu.CompilerParams(
                collective_id=0, has_side_effects=True, vmem_limit_bytes=60 * 1024 * 1024
            ),
        )(
            right_side,
            current_ratio.reshape(1, width),
            filament_xy,
            element_offset,
            element_filament.reshape(elements // LANES, LANES),
            element_order.reshape(elements // LANES, LANES),
        )

    return jax.shard_map(
        on_device,
        mesh=mesh,
        in_specs=(
            P("groups", ("row", "col")),
            P(("groups", "row", "col")),
            P(),
            P(None, "groups"),
            P("groups"),
            P("groups"),
        ),
        out_specs=(P("groups", ("row", "col")), P("groups", ("row", "col"))),
        check_vma=False,
    )
```

```python
import functools
import math

import jax
import jax.numpy as jnp
from jax import lax
from jax.experimental import pallas as pl
from jax.experimental.pallas import tpu as pltpu
from jax.sharding import PartitionSpec as P

EPS_SQUARED = 0.0001
COUPLE = 0.3
LANES = 128
MESH = pl.DeviceIdType.MESH


def loop(count, body):
    if count <= 16:
        for k in range(count):
            body(k)
    else:
        lax.fori_loop(0, count, lambda k, _: (body(k), 0)[1], 0)


def fold(start, stop, body, carry):
    if stop - start <= 16:
        for k in range(start, stop):
            carry = body(k, carry)
        return carry
    return lax.fori_loop(start, stop, body, carry)


def pick(table, index):
    rows, n = table.shape[0], index.shape[1]
    hot = (lax.broadcasted_iota(jnp.int32, (rows, n), 0) == (index >> 7)).astype(jnp.float32)
    taken = lax.dot_general(
        table.T, hot, (((1,), (0,)), ((), ())), precision=lax.Precision.HIGHEST, preferred_element_type=jnp.float32
    )
    lane = lax.broadcasted_iota(jnp.int32, (LANES, n), 0)
    return jnp.sum(jnp.where(lane == (index & (LANES - 1)), taken, 0.0), axis=0, keepdims=True)


def split(value):
    high = value.astype(jnp.bfloat16)
    low = (value - high.astype(jnp.float32)).astype(jnp.bfloat16)
    return high, low


def kernel(
    rows, cols, scale,
    b_hbm, ratio_hbm, xy_hbm, offset_hbm, filament_hbm, order_hbm,
    solution_ref, residual_ref,
    b_ref, ratio_ref, xy_ref, offset_ref, filament_ref, order_ref,
    offset_tab, xy_tab, near, high_all, low_all, b_all, xy_all, image_all, r_all, dots,
    load, send_b, recv_b, send_xy, recv_xy, send_im, recv_im, send_dot, recv_dot,
):
    count = rows * cols
    side, width = b_ref.shape
    group = lax.axis_index("groups")
    row, col = lax.axis_index("row"), lax.axis_index("col")
    me = row * cols + col

    loads = [
        pltpu.make_async_copy(src, dst, load.at[k])
        for k, (src, dst) in enumerate(
            (
                (order_hbm, order_ref), (filament_hbm, filament_ref), (offset_hbm, offset_ref),
                (xy_hbm, xy_ref), (b_hbm, b_ref), (ratio_hbm, ratio_ref),
            )
        )
    ]
    for one in loads:
        one.start()

    def row_at(k):
        return lax.rem(row + k, rows)

    def col_at(c):
        return lax.rem(col + c, cols)

    def device(p):
        return (group, p // cols, lax.rem(p, cols))

    def peer(k):
        return lax.rem(me + k, count)

    def push(src, dst, send, recv, device_id):
        return pltpu.make_async_remote_copy(
            src_ref=src, dst_ref=dst, send_sem=send, recv_sem=recv, device_id=device_id, device_id_type=MESH
        )

    def across(src, dst_all, send, recv, k):
        return push(src, dst_all.at[me], send.at[k], recv.at[me], (group, row_at(k), col))

    def beside(src, dst_all, send, recv, k, c):
        p = row_at(k) * cols + col
        src = dst_all.at[p] if src is None else src
        return push(src, dst_all.at[p], send.at[rows + k * cols + c], recv.at[p], (group, row, col_at(c)))

    def spread(src, dst_all, send, recv):
        loop(rows - 1, lambda k: across(src, dst_all, send, recv, k + 1).start())
        loop(cols - 1, lambda c: beside(src, dst_all, send, recv, 0, c + 1).start())

    def forward(dst_all, send, recv, k):
        arrived(dst_all, recv, row_at(k) * cols + col)
        for c in range(1, cols):
            beside(None, dst_all, send, recv, k, c).start()

    def arrived(dst_all, recv, p):
        push(dst_all.at[p], dst_all.at[p], send_b.at[0], recv.at[p], device(peer(1))).wait_recv()

    def sent(src, dst_all, send, recv):
        loop(rows - 1, lambda k: across(src, dst_all, send, recv, k + 1).wait_send())
        for c in range(1, cols):
            loop(rows, lambda k: beside(None, dst_all, send, recv, k, c).wait_send())

    barrier = pltpu.get_barrier_semaphore()
    loop(count - 1, lambda k: pl.semaphore_signal(barrier, inc=1, device_id=device(peer(k + 1)), device_id_type=MESH))

    for one in loads:
        one.wait()
    for ref, tab in ((offset_ref, offset_tab), (xy_ref, xy_tab)):
        for axis in range(2):
            for q in range(ref.shape[1] // LANES):
                tab[axis, q : q + 1, :] = ref[axis : axis + 1, q * LANES : (q + 1) * LANES]
    parts = width // LANES
    order = jnp.concatenate([order_ref[pl.ds(me * parts + k, 1), :] for k in range(parts)], axis=1)
    filament = (pick(filament_ref[...].astype(jnp.float32), order) + 0.5).astype(jnp.int32)
    places = [pick(xy_tab[axis], filament) + pick(offset_tab[axis], order) for axis in range(2)]
    for axis in range(2):
        xy_all[me, axis : axis + 1, :] = places[axis]
    b_all[me] = b_ref[...]

    for axis in range(2):
        near[axis] = jnp.broadcast_to(places[axis], (width, width)).T
    ratio = ratio_ref[...]
    cube = ratio * ratio * ratio
    sixth = cube * cube
    twelfth = sixth * sixth
    diagonal = 1.0 + 8.0 * (twelfth * twelfth)

    def couple(p):
        dx = near[0] - xy_all[p, 0:1, :]
        dy = near[1] - xy_all[p, 1:2, :]
        high_all[p], low_all[p] = split(lax.rsqrt(dx * dx + dy * dy + EPS_SQUARED))

    def term(p, vector, total):
        v_high, v_low = split(vector)
        contract = (((1,), (1,)), ((), ()))
        both = lax.dot_general(
            jnp.concatenate([v_high, v_low], axis=0), high_all[p], contract, preferred_element_type=jnp.float32
        )
        rest = lax.dot_general(v_high, low_all[p], contract, preferred_element_type=jnp.float32)
        return total + both[:side] + (both[side:] + rest)

    couple(me)
    pl.semaphore_wait(barrier, count - 1)
    spread(xy_all.at[me], xy_all, send_xy, recv_xy)
    spread(b_ref, b_all, send_b, recv_b)

    zero = jnp.zeros((side, width), jnp.float32)

    def rowsum(value):
        return jnp.sum(value, axis=1, keepdims=True)

    def other(k):
        return row_at(k // (cols - 1)) * cols + col_at(1 + lax.rem(k, cols - 1))

    others = rows * (cols - 1)

    b = b_ref[...]
    total = term(me, b, zero)

    def gather_xy(k, carry):
        forward(xy_all, send_xy, recv_xy, k)
        couple(row_at(k) * cols + col)
        return carry

    def gather_b(k, carry):
        forward(b_all, send_b, recv_b, k)
        return carry

    def couple_other(k, carry):
        p = other(k)
        arrived(xy_all, recv_xy, p)
        couple(p)
        return carry

    def add_first(p, carry):
        total, squares = carry
        value = b_all[p]
        return term(p, value, total), squares + value * value

    def first(k, carry):
        return add_first(row_at(k) * cols + col, carry)

    def first_other(k, carry):
        p = other(k)
        arrived(b_all, recv_b, p)
        return add_first(p, carry)

    lax.fori_loop(1, rows, gather_xy, 0)
    couple_other(0, 0)
    lax.fori_loop(1, rows, lambda k, carry: couple_other(k, gather_b(k, carry)), 0)
    lax.fori_loop(rows, others, couple_other, 0)
    carry = fold(1, rows, first, (total, b * b))
    total, squares = fold(0, others, first_other, carry)
    image = diagonal * b + scale * total
    image_all[me] = image
    spread(image_all.at[me], image_all, send_im, recv_im)
    norm = rowsum(squares)

    def curve(k, carry):
        forward(image_all, send_im, recv_im, k)
        p = row_at(k) * cols + col
        return carry + b_all[p] * image_all[p]

    def curve_other(k, carry):
        p = other(k)
        arrived(image_all, recv_im, p)
        return carry + b_all[p] * image_all[p]

    carry = lax.fori_loop(1, rows, curve, b * image)
    curved = rowsum(lax.fori_loop(0, others, curve_other, carry))
    step = norm / curved

    def reduce_residual(k, carry):
        value = b_all[k] - step * image_all[k]
        r_all[k] = value
        return carry + value * value

    norm_next = rowsum(fold(0, count, reduce_residual, zero))
    beta = norm_next / norm

    def second(k, total):
        return term(k, r_all[k] + beta * b_all[k], total)

    total = fold(0, count, second, zero)
    residual = r_all[me]
    direction = residual + beta * b
    image2 = diagonal * direction + scale * total

    own = (
        lax.broadcasted_iota(jnp.int32, (side, LANES), 0) == lax.broadcasted_iota(jnp.int32, (side, LANES), 1)
    )
    partial = rowsum(direction * image2)
    dots[me] = jnp.sum(jnp.where(own, partial, 0.0), axis=0, keepdims=True)

    def give(k):
        return push(dots.at[me], dots.at[me], send_dot.at[k], recv_dot.at[me], device(peer(k)))

    loop(count - 1, lambda k: give(k + 1).start())
    loop(count - 1, lambda k: arrived(dots, recv_dot, peer(k + 1)))
    flat = lax.fori_loop(0, count, lambda k, acc: acc + dots[k], jnp.zeros((1, LANES), jnp.float32))
    curved2 = rowsum(jnp.where(own, flat, 0.0))
    step2 = norm_next / curved2
    solution_ref[...] = step * b + step2 * direction
    residual_ref[...] = residual - step2 * image2

    sent(b_ref, b_all, send_b, recv_b)
    sent(xy_all.at[me], xy_all, send_xy, recv_xy)
    sent(image_all.at[me], image_all, send_im, recv_im)
    loop(count - 1, lambda k: give(k + 1).wait_send())


def solution(mesh):
    rows, cols = mesh.shape["row"], mesh.shape["col"]
    count = rows * cols

    def on_device(right_side, current_ratio, filament_xy, element_offset, element_filament, element_order):
        side, width = right_side.shape
        elements = width * count
        shape = jax.ShapeDtypeStruct((side, width), jnp.float32)
        vmem = pl.BlockSpec(memory_space=pltpu.VMEM)
        f32 = jnp.float32
        blocks = pltpu.VMEM((count, side, width), f32)
        return pl.pallas_call(
            functools.partial(kernel, rows, cols, COUPLE / math.sqrt(elements)),
            out_shape=(shape, shape),
            in_specs=[pl.BlockSpec(memory_space=pltpu.HBM)] * 6,
            out_specs=(vmem, vmem),
            scratch_shapes=[
                pltpu.VMEM((side, width), f32),
                pltpu.VMEM((1, width), f32),
                pltpu.VMEM(filament_xy.shape, f32),
                pltpu.VMEM(element_offset.shape, f32),
                pltpu.VMEM((elements // LANES, LANES), jnp.int32),
                pltpu.VMEM((elements // LANES, LANES), jnp.int32),
                pltpu.VMEM((2, elements // LANES, LANES), f32),
                pltpu.VMEM((2, filament_xy.shape[1] // LANES, LANES), f32),
                pltpu.VMEM((2, width, width), f32),
                pltpu.VMEM((count, width, width), jnp.bfloat16),
                pltpu.VMEM((count, width, width), jnp.bfloat16),
                blocks,
                pltpu.VMEM((count, 2, width), f32),
                blocks,
                blocks,
                pltpu.VMEM((count, 1, LANES), f32),
            ]
            + [pltpu.SemaphoreType.DMA((6,))]
            + [pltpu.SemaphoreType.DMA((rows * (1 + cols),)), pltpu.SemaphoreType.DMA((count,))] * 4,
            compiler_params=pltpu.CompilerParams(
                collective_id=0, has_side_effects=True, vmem_limit_bytes=60 * 1024 * 1024
            ),
        )(
            right_side,
            current_ratio.reshape(1, width),
            filament_xy,
            element_offset,
            element_filament.reshape(elements // LANES, LANES),
            element_order.reshape(elements // LANES, LANES),
        )

    return jax.shard_map(
        on_device,
        mesh=mesh,
        in_specs=(
            P("groups", ("row", "col")),
            P(("groups", "row", "col")),
            P(),
            P(None, "groups"),
            P("groups"),
            P("groups"),
        ),
        out_specs=(P("groups", ("row", "col")), P("groups", ("row", "col"))),
        check_vma=False,
    )
```

```python
import functools
import math

import jax
import jax.numpy as jnp
from jax import lax
from jax.experimental import pallas as pl
from jax.experimental.pallas import tpu as pltpu
from jax.sharding import PartitionSpec as P

EPS_SQUARED = 0.0001
COUPLE = 0.3
LANES = 128
MESH = pl.DeviceIdType.MESH


def loop(count, body):
    if count <= 16:
        for k in range(count):
            body(k)
    else:
        lax.fori_loop(0, count, lambda k, _: (body(k), 0)[1], 0)


def fold(start, stop, body, carry):
    if stop - start <= 16:
        for k in range(start, stop):
            carry = body(k, carry)
        return carry
    return lax.fori_loop(start, stop, body, carry)


def pick(table, index):
    rows, n = table.shape[0], index.shape[1]
    hot = (lax.broadcasted_iota(jnp.int32, (rows, n), 0) == (index >> 7)).astype(jnp.float32)
    taken = lax.dot_general(
        table.T, hot, (((1,), (0,)), ((), ())), precision=lax.Precision.HIGHEST, preferred_element_type=jnp.float32
    )
    lane = lax.broadcasted_iota(jnp.int32, (LANES, n), 0)
    return jnp.sum(jnp.where(lane == (index & (LANES - 1)), taken, 0.0), axis=0, keepdims=True)


def split(value):
    high = value.astype(jnp.bfloat16)
    low = (value - high.astype(jnp.float32)).astype(jnp.bfloat16)
    return high, low


def kernel(
    rows, cols, scale,
    b_hbm, ratio_hbm, xy_hbm, offset_hbm, filament_hbm, order_hbm,
    out_ref,
    b_ref, ratio_ref, xy_ref, offset_ref, filament_ref, order_ref,
    offset_tab, xy_tab, near, high_all, low_all, b_all, xy_all, image_all, dots,
    load, send_b, recv_b, send_xy, recv_xy, send_im, recv_im, send_dot, recv_dot,
):
    count = rows * cols
    side, width = b_ref.shape
    group = lax.axis_index("groups")
    row, col = lax.axis_index("row"), lax.axis_index("col")
    me = row * cols + col

    loads = [
        pltpu.make_async_copy(src, dst, load.at[k])
        for k, (src, dst) in enumerate(
            (
                (order_hbm, order_ref), (filament_hbm, filament_ref), (offset_hbm, offset_ref),
                (xy_hbm, xy_ref), (b_hbm, b_ref), (ratio_hbm, ratio_ref),
            )
        )
    ]
    for one in loads:
        one.start()

    def row_at(k):
        return lax.rem(row + k, rows)

    def col_at(c):
        return lax.rem(col + c, cols)

    def device(p):
        return (group, p // cols, lax.rem(p, cols))

    def peer(k):
        return lax.rem(me + k, count)

    def push(src, dst, send, recv, device_id):
        return pltpu.make_async_remote_copy(
            src_ref=src, dst_ref=dst, send_sem=send, recv_sem=recv, device_id=device_id, device_id_type=MESH
        )

    def across(src, dst_all, send, recv, k):
        return push(src, dst_all.at[me], send.at[k], recv.at[me], (group, row_at(k), col))

    def beside(src, dst_all, send, recv, k, c):
        p = row_at(k) * cols + col
        src = dst_all.at[p] if src is None else src
        return push(src, dst_all.at[p], send.at[rows + k * cols + c], recv.at[p], (group, row, col_at(c)))

    def spread(src, dst_all, send, recv):
        loop(rows - 1, lambda k: across(src, dst_all, send, recv, k + 1).start())
        loop(cols - 1, lambda c: beside(src, dst_all, send, recv, 0, c + 1).start())

    def forward(dst_all, send, recv, k):
        arrived(dst_all, recv, row_at(k) * cols + col)
        for c in range(1, cols):
            beside(None, dst_all, send, recv, k, c).start()

    def arrived(dst_all, recv, p):
        push(dst_all.at[p], dst_all.at[p], send_b.at[0], recv.at[p], device(peer(1))).wait_recv()

    def sent(src, dst_all, send, recv):
        loop(rows - 1, lambda k: across(src, dst_all, send, recv, k + 1).wait_send())
        for c in range(1, cols):
            loop(rows, lambda k: beside(None, dst_all, send, recv, k, c).wait_send())

    barrier = pltpu.get_barrier_semaphore()
    loop(count - 1, lambda k: pl.semaphore_signal(barrier, inc=1, device_id=device(peer(k + 1)), device_id_type=MESH))

    for one in loads:
        one.wait()
    for ref, tab in ((offset_ref, offset_tab), (xy_ref, xy_tab)):
        for axis in range(2):
            for q in range(ref.shape[1] // LANES):
                tab[axis, q : q + 1, :] = ref[axis : axis + 1, q * LANES : (q + 1) * LANES]
    parts = width // LANES
    order = jnp.concatenate([order_ref[pl.ds(me * parts + k, 1), :] for k in range(parts)], axis=1)
    filament = (pick(filament_ref[...].astype(jnp.float32), order) + 0.5).astype(jnp.int32)
    places = [pick(xy_tab[axis], filament) + pick(offset_tab[axis], order) for axis in range(2)]
    for axis in range(2):
        xy_all[me, axis : axis + 1, :] = places[axis]
    b_all[me] = b_ref[...]

    for axis in range(2):
        near[axis] = jnp.broadcast_to(places[axis], (width, width)).T
    ratio = ratio_ref[...]
    cube = ratio * ratio * ratio
    sixth = cube * cube
    twelfth = sixth * sixth
    diagonal = 1.0 + 8.0 * (twelfth * twelfth)

    def couple(p):
        dx = near[0] - xy_all[p, 0:1, :]
        dy = near[1] - xy_all[p, 1:2, :]
        high_all[p], low_all[p] = split(lax.rsqrt(dx * dx + dy * dy + EPS_SQUARED))

    def term(p, vector, total):
        v_high, v_low = split(vector)
        contract = (((1,), (1,)), ((), ()))
        both = lax.dot_general(
            jnp.concatenate([v_high, v_low], axis=0), high_all[p], contract, preferred_element_type=jnp.float32
        )
        rest = lax.dot_general(v_high, low_all[p], contract, preferred_element_type=jnp.float32)
        return total + both[:side] + (both[side:] + rest)

    couple(me)
    pl.semaphore_wait(barrier, count - 1)
    spread(xy_all.at[me], xy_all, send_xy, recv_xy)
    spread(b_ref, b_all, send_b, recv_b)

    zero = jnp.zeros((side, width), jnp.float32)

    def rowsum(value):
        return jnp.sum(value, axis=1, keepdims=True)

    def other(k):
        return row_at(k // (cols - 1)) * cols + col_at(1 + lax.rem(k, cols - 1))

    others = rows * (cols - 1)

    b = b_ref[...]
    total = term(me, b, zero)

    def gather_xy(k, carry):
        forward(xy_all, send_xy, recv_xy, k)
        couple(row_at(k) * cols + col)
        return carry

    def gather_b(k, carry):
        forward(b_all, send_b, recv_b, k)
        return carry

    def couple_other(k, carry):
        p = other(k)
        arrived(xy_all, recv_xy, p)
        couple(p)
        return carry

    def add_first(p, carry):
        total, squares = carry
        value = b_all[p]
        return term(p, value, total), squares + value * value

    def first(k, carry):
        return add_first(row_at(k) * cols + col, carry)

    def first_other(k, carry):
        p = other(k)
        arrived(b_all, recv_b, p)
        return add_first(p, carry)

    lax.fori_loop(1, rows, gather_xy, 0)
    couple_other(0, 0)
    lax.fori_loop(1, rows, lambda k, carry: couple_other(k, gather_b(k, carry)), 0)
    lax.fori_loop(rows, others, couple_other, 0)
    carry = fold(1, rows, first, (total, b * b))
    total, squares = fold(0, others, first_other, carry)
    image = diagonal * b + scale * total
    image_all[me] = image
    spread(image_all.at[me], image_all, send_im, recv_im)
    norm = rowsum(squares)

    def add_image(p, carry):
        turned, products = carry
        value = image_all[p]
        return term(p, value, turned), products + b_all[p] * value

    def curve(k, carry):
        forward(image_all, send_im, recv_im, k)
        return add_image(row_at(k) * cols + col, carry)

    def curve_other(k, carry):
        p = other(k)
        arrived(image_all, recv_im, p)
        return add_image(p, carry)

    carry = fold(1, rows, curve, (term(me, image, zero), b * image))
    turned, products = fold(0, others, curve_other, carry)
    step = norm / rowsum(products)

    def residual_squares(k, carry):
        value = b_all[k] - step * image_all[k]
        return carry + value * value

    norm_next = rowsum(fold(0, count, residual_squares, zero))
    beta = norm_next / norm
    residual = b - step * image
    direction = residual + beta * b
    image2 = diagonal * direction + scale * ((1.0 + beta) * total - step * turned)

    own = (
        lax.broadcasted_iota(jnp.int32, (side, LANES), 0) == lax.broadcasted_iota(jnp.int32, (side, LANES), 1)
    )
    partial = rowsum(direction * image2)
    dots[me] = jnp.sum(jnp.where(own, partial, 0.0), axis=0, keepdims=True)

    def give(k):
        return push(dots.at[me], dots.at[me], send_dot.at[k], recv_dot.at[me], device(peer(k)))

    loop(count - 1, lambda k: give(k + 1).start())
    loop(count - 1, lambda k: arrived(dots, recv_dot, peer(k + 1)))
    flat = lax.fori_loop(0, count, lambda k, acc: acc + dots[k], jnp.zeros((1, LANES), jnp.float32))
    curved2 = rowsum(jnp.where(own, flat, 0.0))
    step2 = norm_next / curved2
    out_ref[0] = step * b + step2 * direction
    out_ref[1] = residual - step2 * image2

    sent(b_ref, b_all, send_b, recv_b)
    sent(xy_all.at[me], xy_all, send_xy, recv_xy)
    sent(image_all.at[me], image_all, send_im, recv_im)
    loop(count - 1, lambda k: give(k + 1).wait_send())


def solution(mesh):
    rows, cols = mesh.shape["row"], mesh.shape["col"]
    count = rows * cols

    def on_device(right_side, current_ratio, filament_xy, element_offset, element_filament, element_order):
        side, width = right_side.shape
        elements = width * count
        shape = jax.ShapeDtypeStruct((2, side, width), jnp.float32)
        vmem = pl.BlockSpec(memory_space=pltpu.VMEM)
        f32 = jnp.float32
        blocks = pltpu.VMEM((count, side, width), f32)
        out = pl.pallas_call(
            functools.partial(kernel, rows, cols, COUPLE / math.sqrt(elements)),
            out_shape=shape,
            in_specs=[pl.BlockSpec(memory_space=pltpu.HBM)] * 6,
            out_specs=vmem,
            scratch_shapes=[
                pltpu.VMEM((side, width), f32),
                pltpu.VMEM((1, width), f32),
                pltpu.VMEM(filament_xy.shape, f32),
                pltpu.VMEM(element_offset.shape, f32),
                pltpu.VMEM((elements // LANES, LANES), jnp.int32),
                pltpu.VMEM((elements // LANES, LANES), jnp.int32),
                pltpu.VMEM((2, elements // LANES, LANES), f32),
                pltpu.VMEM((2, filament_xy.shape[1] // LANES, LANES), f32),
                pltpu.VMEM((2, width, width), f32),
                pltpu.VMEM((count, width, width), jnp.bfloat16),
                pltpu.VMEM((count, width, width), jnp.bfloat16),
                blocks,
                pltpu.VMEM((count, 2, width), f32),
                blocks,
                pltpu.VMEM((count, 1, LANES), f32),
            ]
            + [pltpu.SemaphoreType.DMA((6,))]
            + [pltpu.SemaphoreType.DMA((rows * (1 + cols),)), pltpu.SemaphoreType.DMA((count,))] * 4,
            compiler_params=pltpu.CompilerParams(
                collective_id=0, has_side_effects=True, vmem_limit_bytes=60 * 1024 * 1024
            ),
        )(
            right_side,
            current_ratio.reshape(1, width),
            filament_xy,
            element_offset,
            element_filament.reshape(elements // LANES, LANES),
            element_order.reshape(elements // LANES, LANES),
        )

        return out[0], out[1]

    return jax.shard_map(
        on_device,
        mesh=mesh,
        in_specs=(
            P("groups", ("row", "col")),
            P(("groups", "row", "col")),
            P(),
            P(None, "groups"),
            P("groups"),
            P("groups"),
        ),
        out_specs=(P("groups", ("row", "col")), P("groups", ("row", "col"))),
        check_vma=False,
    )
```

```python
import functools
import math

import jax
import jax.numpy as jnp
from jax import lax
from jax.experimental import pallas as pl
from jax.experimental.pallas import tpu as pltpu
from jax.sharding import PartitionSpec as P

EPS_SQUARED = 0.0001
COUPLE = 0.3
LANES = 128
MESH = pl.DeviceIdType.MESH


def loop(count, body):
    if count <= 16:
        for k in range(count):
            body(k)
    else:
        lax.fori_loop(0, count, lambda k, _: (body(k), 0)[1], 0)


def fold(start, stop, body, carry):
    if stop - start <= 16:
        for k in range(start, stop):
            carry = body(k, carry)
        return carry
    return lax.fori_loop(start, stop, body, carry)


def pick(table, index):
    rows, n = table.shape[0], index.shape[1]
    hot = (lax.broadcasted_iota(jnp.int32, (rows, n), 0) == (index >> 7)).astype(jnp.float32)
    taken = lax.dot_general(
        table.T, hot, (((1,), (0,)), ((), ())), precision=lax.Precision.HIGHEST, preferred_element_type=jnp.float32
    )
    lane = lax.broadcasted_iota(jnp.int32, (LANES, n), 0)
    return jnp.sum(jnp.where(lane == (index & (LANES - 1)), taken, 0.0), axis=0, keepdims=True)


def split(value):
    high = value.astype(jnp.bfloat16)
    low = (value - high.astype(jnp.float32)).astype(jnp.bfloat16)
    return high, low


def kernel(
    rows, cols, scale,
    b_hbm, ratio_hbm, xy_hbm, offset_hbm, filament_hbm, order_hbm,
    out_ref,
    b_ref, ratio_ref, xy_ref, offset_ref, filament_ref, order_ref,
    offset_tab, xy_tab, near, high_all, low_all, b_all, xy_all, image_all, dots,
    load, send_b, recv_b, send_xy, recv_xy, send_im, recv_im, send_dot, recv_dot,
):
    count = rows * cols
    side, width = b_ref.shape
    group = lax.axis_index("groups")
    row, col = lax.axis_index("row"), lax.axis_index("col")
    me = row * cols + col

    loads = [
        pltpu.make_async_copy(src, dst, load.at[k])
        for k, (src, dst) in enumerate(
            (
                (order_hbm, order_ref), (filament_hbm, filament_ref), (offset_hbm, offset_ref),
                (xy_hbm, xy_ref), (b_hbm, b_ref), (ratio_hbm, ratio_ref),
            )
        )
    ]
    for one in loads:
        one.start()

    def row_at(k):
        return lax.rem(row + k, rows)

    def col_at(c):
        return lax.rem(col + c, cols)

    def device(p):
        return (group, p // cols, lax.rem(p, cols))

    def peer(k):
        return lax.rem(me + k, count)

    def push(src, dst, send, recv, device_id):
        return pltpu.make_async_remote_copy(
            src_ref=src, dst_ref=dst, send_sem=send, recv_sem=recv, device_id=device_id, device_id_type=MESH
        )

    def across(src, dst_all, send, recv, k):
        return push(src, dst_all.at[me], send.at[k], recv.at[me], (group, row_at(k), col))

    def beside(src, dst_all, send, recv, k, c):
        p = row_at(k) * cols + col
        src = dst_all.at[p] if src is None else src
        return push(src, dst_all.at[p], send.at[rows + k * cols + c], recv.at[p], (group, row, col_at(c)))

    def spread(src, dst_all, send, recv):
        loop(cols - 1, lambda c: beside(src, dst_all, send, recv, 0, c + 1).start())
        loop(rows - 1, lambda k: across(src, dst_all, send, recv, 1 + (k + rows // 2 - 1) % (rows - 1)).start())

    def forward(dst_all, send, recv, k):
        arrived(dst_all, recv, row_at(k) * cols + col)
        for c in range(1, cols):
            beside(None, dst_all, send, recv, k, c).start()

    def arrived(dst_all, recv, p):
        push(dst_all.at[p], dst_all.at[p], send_b.at[0], recv.at[p], device(peer(1))).wait_recv()

    def sent(src, dst_all, send, recv):
        loop(rows - 1, lambda k: across(src, dst_all, send, recv, k + 1).wait_send())
        for c in range(1, cols):
            loop(rows, lambda k: beside(None, dst_all, send, recv, k, c).wait_send())

    barrier = pltpu.get_barrier_semaphore()
    loop(count - 1, lambda k: pl.semaphore_signal(barrier, inc=1, device_id=device(peer(k + 1)), device_id_type=MESH))

    for one in loads:
        one.wait()
    for ref, tab in ((offset_ref, offset_tab), (xy_ref, xy_tab)):
        for axis in range(2):
            for q in range(ref.shape[1] // LANES):
                tab[axis, q : q + 1, :] = ref[axis : axis + 1, q * LANES : (q + 1) * LANES]
    parts = width // LANES
    order = jnp.concatenate([order_ref[pl.ds(me * parts + k, 1), :] for k in range(parts)], axis=1)
    filament = (pick(filament_ref[...].astype(jnp.float32), order) + 0.5).astype(jnp.int32)
    places = [pick(xy_tab[axis], filament) + pick(offset_tab[axis], order) for axis in range(2)]
    for axis in range(2):
        xy_all[me, axis : axis + 1, :] = places[axis]
    b_all[me] = b_ref[...]

    for axis in range(2):
        near[axis] = jnp.broadcast_to(places[axis], (width, width)).T
    ratio = ratio_ref[...]
    cube = ratio * ratio * ratio
    sixth = cube * cube
    twelfth = sixth * sixth
    diagonal = 1.0 + 8.0 * (twelfth * twelfth)

    def couple(p):
        dx = near[0] - xy_all[p, 0:1, :]
        dy = near[1] - xy_all[p, 1:2, :]
        high_all[p], low_all[p] = split(lax.rsqrt(dx * dx + dy * dy + EPS_SQUARED))

    def term(p, vector, total):
        v_high, v_low = split(vector)
        contract = (((1,), (1,)), ((), ()))
        both = lax.dot_general(
            jnp.concatenate([v_high, v_low], axis=0), high_all[p], contract, preferred_element_type=jnp.float32
        )
        rest = lax.dot_general(v_high, low_all[p], contract, preferred_element_type=jnp.float32)
        return total + both[:side] + (both[side:] + rest)

    couple(me)
    pl.semaphore_wait(barrier, count - 1)
    spread(xy_all.at[me], xy_all, send_xy, recv_xy)
    spread(b_ref, b_all, send_b, recv_b)

    zero = jnp.zeros((side, width), jnp.float32)

    def rowsum(value):
        return jnp.sum(value, axis=1, keepdims=True)

    def other(k):
        return row_at(k // (cols - 1)) * cols + col_at(1 + lax.rem(k, cols - 1))

    others = rows * (cols - 1)

    b = b_ref[...]
    total = term(me, b, zero)

    def gather_xy(k, carry):
        forward(xy_all, send_xy, recv_xy, k)
        couple(row_at(k) * cols + col)
        return carry

    def gather_b(k, carry):
        forward(b_all, send_b, recv_b, k)
        return carry

    def couple_other(k, carry):
        p = other(k)
        arrived(xy_all, recv_xy, p)
        couple(p)
        return carry

    def add_first(p, carry):
        total, squares = carry
        value = b_all[p]
        return term(p, value, total), squares + value * value

    def first(k, carry):
        return add_first(row_at(k) * cols + col, carry)

    def first_other(k, carry):
        p = other(k)
        arrived(b_all, recv_b, p)
        return add_first(p, carry)

    fold(1, rows, gather_xy, 0)
    couple_other(0, 0)
    fold(1, rows, lambda k, carry: couple_other(k, gather_b(k, carry)), 0)
    lax.fori_loop(rows, others, couple_other, 0)
    carry = fold(1, rows, first, (total, b * b))
    total, squares = fold(0, others, first_other, carry)
    image = diagonal * b + scale * total
    image_all[me] = image
    spread(image_all.at[me], image_all, send_im, recv_im)
    norm = rowsum(squares)

    def add_image(p, carry):
        turned, products = carry
        value = image_all[p]
        return term(p, value, turned), products + b_all[p] * value

    def curve(k, carry):
        forward(image_all, send_im, recv_im, k)
        return add_image(row_at(k) * cols + col, carry)

    def curve_other(k, carry):
        p = other(k)
        arrived(image_all, recv_im, p)
        return add_image(p, carry)

    carry = fold(1, rows, curve, (term(me, image, zero), b * image))
    turned, products = fold(0, others, curve_other, carry)
    step = norm / rowsum(products)

    def residual_squares(k, carry):
        value = b_all[k] - step * image_all[k]
        return carry + value * value

    norm_next = rowsum(fold(0, count, residual_squares, zero))
    beta = norm_next / norm
    residual = b - step * image
    direction = residual + beta * b
    image2 = diagonal * direction + scale * ((1.0 + beta) * total - step * turned)

    own = (
        lax.broadcasted_iota(jnp.int32, (side, LANES), 0) == lax.broadcasted_iota(jnp.int32, (side, LANES), 1)
    )
    partial = rowsum(direction * image2)
    dots[me] = jnp.sum(jnp.where(own, partial, 0.0), axis=0, keepdims=True)

    def give(k):
        return push(dots.at[me], dots.at[me], send_dot.at[k], recv_dot.at[me], device(peer(k)))

    loop(count - 1, lambda k: give(1 + (k + count // 2 - 1) % (count - 1)).start())
    loop(count - 1, lambda k: arrived(dots, recv_dot, peer(k + 1)))
    flat = lax.fori_loop(0, count, lambda k, acc: acc + dots[k], jnp.zeros((1, LANES), jnp.float32))
    curved2 = rowsum(jnp.where(own, flat, 0.0))
    step2 = norm_next / curved2
    out_ref[0] = step * b + step2 * direction
    out_ref[1] = residual - step2 * image2

    sent(b_ref, b_all, send_b, recv_b)
    sent(xy_all.at[me], xy_all, send_xy, recv_xy)
    sent(image_all.at[me], image_all, send_im, recv_im)
    loop(count - 1, lambda k: give(k + 1).wait_send())


def solution(mesh):
    rows, cols = mesh.shape["row"], mesh.shape["col"]
    count = rows * cols

    def on_device(right_side, current_ratio, filament_xy, element_offset, element_filament, element_order):
        side, width = right_side.shape
        elements = width * count
        shape = jax.ShapeDtypeStruct((2, side, width), jnp.float32)
        vmem = pl.BlockSpec(memory_space=pltpu.VMEM)
        f32 = jnp.float32
        blocks = pltpu.VMEM((count, side, width), f32)
        out = pl.pallas_call(
            functools.partial(kernel, rows, cols, COUPLE / math.sqrt(elements)),
            out_shape=shape,
            in_specs=[pl.BlockSpec(memory_space=pltpu.HBM)] * 6,
            out_specs=vmem,
            scratch_shapes=[
                pltpu.VMEM((side, width), f32),
                pltpu.VMEM((1, width), f32),
                pltpu.VMEM(filament_xy.shape, f32),
                pltpu.VMEM(element_offset.shape, f32),
                pltpu.VMEM((elements // LANES, LANES), jnp.int32),
                pltpu.VMEM((elements // LANES, LANES), jnp.int32),
                pltpu.VMEM((2, elements // LANES, LANES), f32),
                pltpu.VMEM((2, filament_xy.shape[1] // LANES, LANES), f32),
                pltpu.VMEM((2, width, width), f32),
                pltpu.VMEM((count, width, width), jnp.bfloat16),
                pltpu.VMEM((count, width, width), jnp.bfloat16),
                blocks,
                pltpu.VMEM((count, 2, width), f32),
                blocks,
                pltpu.VMEM((count, 1, LANES), f32),
            ]
            + [pltpu.SemaphoreType.DMA((6,))]
            + [pltpu.SemaphoreType.DMA((rows * (1 + cols),)), pltpu.SemaphoreType.DMA((count,))] * 4,
            compiler_params=pltpu.CompilerParams(
                collective_id=0, has_side_effects=True, vmem_limit_bytes=60 * 1024 * 1024
            ),
        )(
            right_side,
            current_ratio.reshape(1, width),
            filament_xy,
            element_offset,
            element_filament.reshape(elements // LANES, LANES),
            element_order.reshape(elements // LANES, LANES),
        )

        return out[0], out[1]

    return jax.shard_map(
        on_device,
        mesh=mesh,
        in_specs=(
            P("groups", ("row", "col")),
            P(("groups", "row", "col")),
            P(),
            P(None, "groups"),
            P("groups"),
            P("groups"),
        ),
        out_specs=(P("groups", ("row", "col")), P("groups", ("row", "col"))),
        check_vma=False,
    )
```
